32 devices in a mesh: scan: 8 (over z, y), cad: 4 (over x, core).
Axes of the slice: x: 2, y: 2, z: 4, core: 2. Of those that a mesh axis runs over, the one named last changes fastest.
Arguments:
- points: float32 [3, 8, 8192], P(None, 'scan', 'cad'), may hold values from -12 to 12
- triangles: float32 [9, 4, 8192], P(None, 'cad', 'scan'), may hold values from -14 to 14, as said below
- point_count: int32 [8, 32], P('scan', 'cad'), may hold values from 1 to 256, as said below
- pairs: int32 [8, 4, 2, 512], P('scan', 'cad'), may hold values from 0 to 63, as said below
- pair_count: int32 [8, 4], P('scan', 'cad'), may hold values from 16 to 512, as said below
Outputs:
- point_min: float32 [8, 8192], P('scan', 'cad')
- tri_min: float32 [4, 8192], P('cad', 'scan')
The draws below stay inside these ranges and needn't reach their ends.
Inputs may be any that keep to these rules, and one draw needn't show every extreme that they name: `point_count`: each point block numbers 256 slots; between 1 and 256 of them are valid. For k < pair_count[s, c], pairs[s, c, 0, k] is below 8 * 4 and pairs[s, c, 1, k] below 8 * 8; slots from pair_count[s, c] on are ignored. Every point block of every scan shard and every triangle block of every cad shard is named by some listed pair. `pair_count`: listed pairs of one device; some device has 512. `triangles`: edges b - a and c - a have squared length 0.0625 or more, edge c - b has squared length 0.005 or more, and every n = e0 x (c - a) has n . n of 0.0005 or more.
All inputs are finite; a program needn't handle non-finite values.
Results may differ from the reference program's by a relative error of at most 0.0003.
Values sent between devices are 32-bit elements; how exact they have to be, the bound alone decides.
A program may use at most 64 MiB of HBM per device.

```python
import jax
import jax.numpy as jnp
from jax import lax

PBLK = 256
TBLK = 128
PB_DEV = 8
TB_DEV = 8
MAXP = 512
PS = 8192
TS = 8192
N_SCAN = 8
N_CAD = 4


def draw_triangles(key, part):
    keys = jax.random.split(jax.random.fold_in(key, 11), 5)
    shape = (N_CAD, TS)
    base = jnp.clip(3.0 * jax.random.normal(keys[0], (3,) + shape, jnp.float32), -12.0, 12.0)
    lengths = jax.random.uniform(keys[2], (2,) + shape, jnp.float32, 0.5, 1.2)
    tilts = jax.random.uniform(keys[3], (4,) + shape, jnp.float32, -0.4, 0.4)
    edge_one = jnp.stack([lengths[0], tilts[0], tilts[1]])
    edge_two = jnp.stack([tilts[2], lengths[1], tilts[3]])
    turns = jax.random.randint(keys[4], shape, 0, 3)

    def rotated(vector):
        once = jnp.stack([vector[1], vector[2], vector[0]])
        twice = jnp.stack([vector[2], vector[0], vector[1]])
        return jnp.where(turns[None] == 0, vector, jnp.where(turns[None] == 1, once, twice))
    vertex_b = base + rotated(edge_one)
    vertex_c = base + rotated(edge_two)
    return jnp.concatenate([base, vertex_b, vertex_c], axis=0).astype(jnp.float32)


def draw_point_count(key, part):
    keys = jax.random.split(jax.random.fold_in(key, 31), 3)
    total = N_SCAN * N_CAD * PB_DEV
    counts = jax.random.randint(keys[0], (total,), 1, PBLK + 1)
    fullest = jax.random.randint(keys[1], (), 0, total)
    emptiest = (fullest + 1 + jax.random.randint(keys[2], (), 0, total - 1)) % total
    counts = counts.at[fullest].set(PBLK).at[emptiest].set(1)
    return counts.reshape(N_SCAN, N_CAD * PB_DEV).astype(jnp.int32)


def pair_plan(key):
    keys = jax.random.split(jax.random.fold_in(key, 23), 4)
    shape = (N_SCAN, N_CAD, MAXP)
    slot_grid = jnp.broadcast_to(jnp.arange(MAXP, dtype=jnp.int32)[None, None, :], shape)
    scan_grid = jnp.broadcast_to(jnp.arange(N_SCAN, dtype=jnp.int32)[:, None, None], shape)
    cad_grid = jnp.broadcast_to(jnp.arange(N_CAD, dtype=jnp.int32)[None, :, None], shape)
    random_points = jax.random.randint(keys[0], shape, 0, PB_DEV * N_CAD)
    random_tris = jax.random.randint(keys[1], shape, 0, TB_DEV * N_SCAN)
    point_block = jnp.where(slot_grid < PB_DEV, cad_grid * PB_DEV + slot_grid, random_points)
    cover_tris = (slot_grid >= PB_DEV) & (slot_grid < PB_DEV + TB_DEV)
    tri_block = jnp.where(cover_tris, scan_grid * TB_DEV + slot_grid - PB_DEV, random_tris)
    table = jnp.stack([point_block, tri_block], axis=2).astype(jnp.int32)
    halving = jax.random.randint(keys[2], (N_SCAN * N_CAD,), 0, 4)
    busiest = jax.random.randint(keys[3], (), 0, N_SCAN * N_CAD)
    halving = halving.at[busiest].set(0)
    counts = jnp.maximum(PB_DEV + TB_DEV, MAXP // jnp.left_shift(1, halving))
    return (table, counts.reshape(N_SCAN, N_CAD).astype(jnp.int32))


def draw_pairs(key, part):
    return pair_plan(key)[0]


def draw_pair_count(key, part):
    return pair_plan(key)[1]


def levels(stream_key, extent, cuts, least, top_value):
    gain, own = 1.0, jax.random.fold_in(stream_key, 6)
    for dim, shards_of in cuts:
        steps = jnp.exp(jax.random.uniform(jax.random.fold_in(own, dim), (shards_of,), jnp.float32, least / len(cuts), top_value / len(cuts)))
        gain = gain * jnp.repeat(steps, extent[dim] // shards_of).reshape([-1 if axis == dim else 1 for axis in range(len(extent))])
    return gain


def gaussian(stream_key, shape, width, bound, cuts=(), kind=jnp.bfloat16):
    drawn = jax.random.normal(stream_key, shape, jnp.float32) * width
    if len(cuts) > 0:
        drawn = levels(stream_key, shape, cuts, -0.22, 0.18) * drawn
    return jnp.clip(drawn, min=-bound, max=bound).astype(kind)


def setup_inputs(seed: int = 0) -> dict:
    key_list = jax.random.split(jax.random.key(seed), 6)
    points = gaussian(key_list[0], (3, N_SCAN, PS), 3.0, 12.0, ((1, 8), (2, 4)), jnp.float32)
    triangles = draw_triangles(jax.random.fold_in(key_list[5], 71), 0)
    point_count = draw_point_count(jax.random.fold_in(key_list[5], 71), 0)
    pairs = draw_pairs(jax.random.fold_in(key_list[5], 71), 0)
    pair_count = draw_pair_count(jax.random.fold_in(key_list[5], 71), 0)
    return dict(points=points, triangles=triangles, point_count=point_count, pairs=pairs, pair_count=pair_count)


far_value = 1.0e30


def cross_product(left_vec, right_vec):
    return (left_vec[1] * right_vec[2] - left_vec[2] * right_vec[1],
            left_vec[2] * right_vec[0] - left_vec[0] * right_vec[2],
            left_vec[0] * right_vec[1] - left_vec[1] * right_vec[0])


def inner_product(left_vec, right_vec):
    return left_vec[0] * right_vec[0] + left_vec[1] * right_vec[1] + left_vec[2] * right_vec[2]


def difference(left_vec, right_vec):
    return (left_vec[0] - right_vec[0], left_vec[1] - right_vec[1], left_vec[2] - right_vec[2])


def as_rows(vector):
    return (vector[0][None, :], vector[1][None, :], vector[2][None, :])


def block_distance(point_block, tri_block):
    vertex_a = (tri_block[0], tri_block[1], tri_block[2])
    vertex_b = (tri_block[3], tri_block[4], tri_block[5])
    vertex_c = (tri_block[6], tri_block[7], tri_block[8])
    edge_ab = difference(vertex_b, vertex_a)
    edge_bc = difference(vertex_c, vertex_b)
    edge_ca = difference(vertex_a, vertex_c)
    normal = cross_product(edge_ab, difference(vertex_c, vertex_a))
    inv_normal = 1.0 / inner_product(normal, normal)
    coords = (point_block[0][:, None], point_block[1][:, None], point_block[2][:, None])

    def edge_terms(anchor, edge):
        inverse = 1.0 / inner_product(edge, edge)
        inward = cross_product(normal, edge)
        offset = difference(coords, as_rows(anchor))
        edge_rows = as_rows(edge)
        along = jnp.clip(inner_product(offset, edge_rows) * inverse[None, :], 0.0, 1.0)
        gap = (offset[0] - along * edge_rows[0], offset[1] - along * edge_rows[1], offset[2] - along * edge_rows[2])
        return inner_product(gap, gap), inner_product(offset, as_rows(inward)), offset

    dist_ab, side_ab, offset_a = edge_terms(vertex_a, edge_ab)
    dist_bc, side_bc, offset_b = edge_terms(vertex_b, edge_bc)
    dist_ca, side_ca, offset_c = edge_terms(vertex_c, edge_ca)
    height = inner_product(offset_a, as_rows(normal))
    plane = height * height * inv_normal[None, :]
    inside = (side_ab >= 0.0) & (side_bc >= 0.0) & (side_ca >= 0.0)
    return jnp.where(inside, plane, jnp.minimum(jnp.minimum(dist_ab, dist_bc), dist_ca))


def reference(points, triangles, point_count, pairs, pair_count):
    zero = jnp.int32(0)
    slots = jnp.arange(PBLK, dtype=jnp.int32)
    valid = (slots[None, None, :] < point_count[:, :, None]).reshape(N_SCAN, PS)
    point_init = jnp.full((N_SCAN, PS), far_value, dtype=jnp.float32)
    tri_init = jnp.full((N_CAD, TS), far_value, dtype=jnp.float32)

    def visit(running, flat):
        scan_ix = (flat // (N_CAD * MAXP)).astype(jnp.int32)
        cad_ix = ((flat // MAXP) % N_CAD).astype(jnp.int32)
        slot_ix = (flat % MAXP).astype(jnp.int32)

        def work(current):
            point_mins, tri_mins = current
            point_start = (pairs[scan_ix, cad_ix, 0, slot_ix] * PBLK).astype(jnp.int32)
            tri_start = (pairs[scan_ix, cad_ix, 1, slot_ix] * TBLK).astype(jnp.int32)
            point_block = lax.dynamic_slice(points, (zero, scan_ix, point_start), (3, 1, PBLK))[:, 0]
            tri_block = lax.dynamic_slice(triangles, (zero, cad_ix, tri_start), (9, 1, TBLK))[:, 0]
            live = lax.dynamic_slice(valid, (scan_ix, point_start), (1, PBLK))[0]
            dist = jnp.where(live[:, None], block_distance(point_block, tri_block), far_value)
            old_points = lax.dynamic_slice(point_mins, (scan_ix, point_start), (1, PBLK))
            point_mins = lax.dynamic_update_slice(point_mins, jnp.minimum(old_points, jnp.min(dist, axis=1)[None, :]), (scan_ix, point_start))
            old_tris = lax.dynamic_slice(tri_mins, (cad_ix, tri_start), (1, TBLK))
            tri_mins = lax.dynamic_update_slice(tri_mins, jnp.minimum(old_tris, jnp.min(dist, axis=0)[None, :]), (cad_ix, tri_start))
            return point_mins, tri_mins

        def skip(current):
            return current

        return lax.cond(slot_ix < pair_count[scan_ix, cad_ix], work, skip, running), None

    flats = jnp.arange(N_SCAN * N_CAD * MAXP, dtype=jnp.int32)
    (point_mins, tri_mins), _ = lax.scan(visit, (point_init, tri_init), flats)
    point_min = jnp.where(valid, point_mins, 0.0)
    return point_min, tri_mins
```

```python
import functools

import jax
import jax.numpy as jnp
from jax import lax
from jax.experimental import pallas as pl
from jax.experimental.pallas import tpu as pltpu
from jax.sharding import PartitionSpec as P

PBLK = 256
TBLK = 128
SUB = 8
GROUPS = PBLK // SUB
PACK = 128 // GROUPS
CHUNK = 4

far_value = 1e30
away = 1e4

MESH = pl.DeviceIdType.MESH


def gather_kernel(
    n_scan, n_cad, n_blocks, block_ref, list_ref, all_ref, mask_ref, count_ref,
    lists, scan_send, scan_recv, list_send, list_recv, hi_send, hi_recv, core_send, core_recv, own_sem, own_list_sem,
):
    n_hi = n_cad // 2
    s = lax.axis_index("scan")
    c = lax.axis_index("cad")
    hi = c // 2
    core = c % 2

    def hi_peer(j):
        return lax.rem(hi + j, n_hi) * 2 + core

    sibling = hi * 2 + (1 - core)

    barrier = pltpu.get_barrier_semaphore()
    for k in range(1, n_scan):
        pl.semaphore_signal(barrier, inc=1, device_id=(lax.rem(s + k, n_scan), c), device_id_type=MESH)
    for j in range(1, n_hi):
        pl.semaphore_signal(barrier, inc=1, device_id=(s, hi_peer(j)), device_id_type=MESH)
    pl.semaphore_signal(barrier, inc=1, device_id=(s, sibling), device_id_type=MESH)
    own = pltpu.make_async_copy(block_ref, all_ref.at[c, s], own_sem)
    own.start()
    own_list = pltpu.make_async_copy(list_ref, lists.at[s], own_list_sem)
    own_list.start()
    pl.semaphore_wait(barrier, n_scan - 1 + n_hi - 1 + 1)

    sends = []

    def remote(src, dst, send, recv, device):
        copy = pltpu.make_async_remote_copy(
            src_ref=src, dst_ref=dst, send_sem=send, recv_sem=recv, device_id=device, device_id_type=MESH
        )
        return copy

    scan_copies = []
    for k in range(1, n_scan):
        copy = remote(block_ref, all_ref.at[c, s], scan_send.at[k], scan_recv.at[k], (lax.rem(s + k, n_scan), c))
        copy.start()
        sends.append(copy)
        scan_copies.append(copy)
    hi_copies = {}

    def forward(k, src, source_scan):
        for j in range(1, n_hi):
            copy = remote(
                src, all_ref.at[c, source_scan], hi_send.at[j, k], hi_recv.at[j, k], (s, hi_peer(j))
            )
            copy.start()
            sends.append(copy)
            hi_copies[(j, k)] = copy
        copy = remote(src, all_ref.at[c, source_scan], core_send.at[0, k], core_recv.at[0, k], (s, sibling))
        copy.start()
        sends.append(copy)
        core_copies.append(copy)

    core_copies = []
    forward(0, block_ref, s)
    list_copies = []
    for k in range(1, n_scan):
        copy = remote(list_ref, lists.at[s], list_send.at[k], list_recv.at[k], (lax.rem(s + k, n_scan), c))
        copy.start()
        sends.append(copy)
        list_copies.append(copy)
    for k in range(1, n_scan):
        scan_copies[k - 1].wait_recv()
        source = lax.rem(s + n_scan - k, n_scan)
        forward(k, all_ref.at[c, source], source)

    own_list.wait()
    for copy in list_copies:
        copy.wait_recv()
    n_tri = 8
    first = s * n_tri
    for shard in range(n_scan):
        total = jnp.zeros((n_tri, n_blocks), jnp.float32)
        for part in range(4):
            point_row = lists[shard, part : part + 1, :]
            tri_row = lists[shard, part + 4 : part + 5, :] - first
            points_hot = (lax.broadcasted_iota(jnp.int32, (n_blocks, 128), 0) == point_row).astype(jnp.float32)
            tris_hot = (lax.broadcasted_iota(jnp.int32, (n_tri, 128), 0) == tri_row).astype(jnp.float32)
            total += lax.dot_general(
                tris_hot, points_hot, (((1,), (1,)), ((), ())), preferred_element_type=jnp.float32
            )
        bit = jnp.left_shift(1, lax.broadcasted_iota(jnp.int32, (n_tri, n_blocks), 0))
        bits = jnp.where(total > 0.5, bit, 0)
        mask_ref[shard : shard + 1, :] = jnp.sum(bits, axis=0, keepdims=True)

    for j in range(1, n_hi):
        column = lax.rem(hi + n_hi - j, n_hi) * 2 + core
        for k in range(n_scan):
            hi_copies[(j, k)].wait_recv()
            source = lax.rem(s + n_scan - k, n_scan)
            src = all_ref.at[column, source]
            copy = remote(src, all_ref.at[column, source], core_send.at[j, k], core_recv.at[j, k], (s, sibling))
            copy.start()
            sends.append(copy)
            core_copies.append(copy)
    for copy in core_copies:
        copy.wait_recv()
    own.wait()
    for copy in sends:
        copy.wait_send()
    for column in range(n_cad):
        for shard in range(n_scan):
            row = column * n_scan + shard
            count_ref[row : row + 1, :] = all_ref[column, shard, 6, 0:1, :].astype(jnp.int32)


def reduce_kernel(n_scan, n_cad, part_ref, out_ref, first, held, second, first_send, first_recv, second_send, second_recv):
    s = lax.axis_index("scan")
    c = lax.axis_index("cad")
    barrier = pltpu.get_barrier_semaphore()
    for k in range(1, n_scan):
        pl.semaphore_signal(barrier, inc=1, device_id=(lax.rem(s + k, n_scan), c), device_id_type=MESH)
    for k in range(1, n_cad):
        pl.semaphore_signal(barrier, inc=1, device_id=(s, lax.rem(c + k, n_cad)), device_id_type=MESH)
    pl.semaphore_wait(barrier, n_scan - 1 + n_cad - 1)
    copies = []
    for k in range(1, n_cad):
        column = lax.rem(c + k, n_cad)
        copy = pltpu.make_async_remote_copy(
            src_ref=part_ref.at[column], dst_ref=first.at[k], send_sem=first_send.at[k], recv_sem=first_recv.at[k],
            device_id=(s, column), device_id_type=MESH,
        )
        copy.start()
        copies.append(copy)
    for copy in copies:
        copy.wait_recv()
    total = part_ref[c]
    for k in range(1, n_cad):
        total = jnp.minimum(total, first[k])
    held[...] = total
    later = []
    for k in range(1, n_scan):
        row = lax.rem(s + k, n_scan)
        copy = pltpu.make_async_remote_copy(
            src_ref=held.at[row], dst_ref=second.at[k], send_sem=second_send.at[k], recv_sem=second_recv.at[k],
            device_id=(row, c), device_id_type=MESH,
        )
        copy.start()
        later.append(copy)
    for copy in later:
        copy.wait_recv()
    own = held[s]
    for k in range(1, n_scan):
        own = jnp.minimum(own, second[k])
    out_ref[...] = own
    for copy in copies + later:
        copy.wait_send()


def dot3(left, right):
    return left[0] * right[0] + left[1] * right[1] + left[2] * right[2]


def minus(left, right):
    return [left[i] - right[i] for i in range(3)]


def frame_rows(tri_ref):
    a = [tri_ref[i] for i in range(3)]
    b = [tri_ref[3 + i] for i in range(3)]
    far = [tri_ref[6 + i] for i in range(3)]
    e0 = minus(b, a)
    h = minus(far, a)
    base = jnp.sqrt(dot3(e0, e0))
    u = [x / base for x in e0]
    cx = dot3(h, u)
    h = [h[i] - cx * u[i] for i in range(3)]
    again = dot3(h, u)
    h = [h[i] - again * u[i] for i in range(3)]
    cx = cx + again
    cy = jnp.sqrt(dot3(h, h))
    v = [x / cy for x in h]
    w = [u[1] * v[2] - u[2] * v[1], u[2] * v[0] - u[0] * v[2], u[0] * v[1] - u[1] * v[0]]
    dx = cx - base
    len1 = jnp.sqrt(dx * dx + cy * cy)
    len2 = jnp.sqrt(cx * cx + cy * cy)
    return a + u + v + w + [base, dx / len1, cy / len1, len1, cx / len2, cy / len2, len2]


N_ROWS = 19


def tile_distance(points, rows):
    ax, ay, az, u0, u1, u2, v0, v1, v2, w0, w1, w2, base, d0, d1, len1, f0, f1, len2 = rows
    px, py, pz = points
    px = px - ax
    py = py - ay
    pz = pz - az
    x = px * u0 + py * u1 + pz * u2
    y = px * v0 + py * v1 + pz * v2
    z = px * w0 + py * w1 + pz * w2
    gap0 = x - jnp.minimum(jnp.maximum(x, 0.0), base)
    seg0 = gap0 * gap0 + y * y
    xb = x - base
    along1 = xb * d0 + y * d1
    side1 = y * d0 - xb * d1
    gap1 = along1 - jnp.minimum(jnp.maximum(along1, 0.0), len1)
    seg1 = gap1 * gap1 + side1 * side1
    along2 = x * f0 + y * f1
    side2 = x * f1 - y * f0
    gap2 = along2 - jnp.minimum(jnp.maximum(along2, 0.0), len2)
    seg2 = gap2 * gap2 + side2 * side2
    edges = jnp.minimum(jnp.minimum(seg0, seg1), seg2)
    side = jnp.minimum(jnp.minimum(y, side1), side2)
    return z * z + jnp.where(side >= 0.0, 0.0, edges)


def pairs_kernel(n_scan, n_cad, mask_ref, count_ref, all_ref, tri_ref, part_ref, out_ref, frames, tri_acc):
    for i, row in enumerate(frame_rows(tri_ref)):
        frames[i] = row
    part_ref[...] = jnp.full_like(part_ref, far_value)
    tri_acc[...] = jnp.full_like(tri_acc, far_value)
    lane = lax.broadcasted_iota(jnp.int32, (SUB, 128), 1)

    def per_block(index, carry):
        where = index // 8
        slot = index % 8
        column = where // n_scan
        shard = where % n_scan
        mask = mask_ref[shard, column * 8 + slot]

        @pl.when(mask != 0)
        def _():
            half = slot // PACK
            lane0 = (slot % PACK) * GROUPS
            steps = (count_ref[where, slot] + CHUNK * SUB - 1) // (CHUNK * SUB)
            px = all_ref[where, half]
            py = all_ref[where, 2 + half]
            pz = all_ref[where, 4 + half]

            def spread(step):
                out = []
                for i in range(CHUNK):
                    at = jnp.full((SUB, 128), lane0 + step * CHUNK + i, jnp.int32)
                    out.append(tuple(
                        jnp.take_along_axis(ref, at, axis=1, mode="promise_in_bounds") for ref in (px, py, pz)
                    ))
                return tuple(out)

            def per_tri(state):
                left, nearest = state
                tri = 31 - lax.clz(left)
                rows = [jnp.broadcast_to(frames[i, pl.ds(tri, 1), :], (SUB, 128)) for i in range(N_ROWS)]

                def fold(nearest, dists, step):
                    for i in range(CHUNK):
                        least = jnp.min(dists[i], axis=1, keepdims=True)
                        hit = lane == lane0 + step * CHUNK + i
                        nearest = jnp.where(hit, jnp.minimum(nearest, least), nearest)
                    return nearest

                def body(step, inner):
                    nearest, best, points, dists = inner
                    nearest = fold(nearest, dists, step - 1)
                    fresh = tuple(tile_distance(points[i], rows) for i in range(CHUNK))
                    following = spread(jnp.minimum(step + 1, GROUPS // CHUNK - 1))
                    for i in range(CHUNK):
                        best = jnp.minimum(best, fresh[i])
                    return nearest, best, following, fresh

                none = tuple(jnp.full((SUB, 128), far_value, jnp.float32) for _ in range(CHUNK))
                nearest, best, _, dists = lax.fori_loop(
                    0, steps, body, (nearest, tri_acc[tri], spread(0), none)
                )
                nearest = fold(nearest, dists, steps - 1)
                tri_acc[tri] = best
                return left - jnp.left_shift(1, tri), nearest

            _, nearest = lax.while_loop(
                lambda state: state[0] != 0, per_tri, (mask, part_ref[where, half])
            )
            part_ref[where, half] = nearest

        return carry

    lax.fori_loop(0, n_scan * n_cad * 8, per_block, 0)
    for t in range(8):
        out_ref[t : t + 1, :] = jnp.min(tri_acc[t], axis=0, keepdims=True)


VMEM = pl.BlockSpec(memory_space=pltpu.VMEM)
SMEM = pl.BlockSpec(memory_space=pltpu.SMEM)
DMA = pltpu.SemaphoreType.DMA
LIMIT = 40 * 1024 * 1024


def shards(n_scan, n_cad, points, triangles, point_count, pairs, pair_count):
    share = points.shape[2]
    blocks = share // PBLK
    n_hi = n_cad // 2
    halves = blocks // PACK
    counts = point_count[0]
    valid = jnp.arange(PBLK, dtype=jnp.int32)[None, :] < counts[:, None]
    placed = jnp.where(valid[None], points[:, 0].reshape(3, blocks, PBLK), away)
    placed = placed.reshape(3, halves, PACK, GROUPS, SUB).transpose(0, 1, 4, 2, 3).reshape(3 * halves, SUB, 128)
    count_tile = jnp.zeros((1, SUB, 128), jnp.float32).at[0, :, :blocks].set(counts.astype(jnp.float32)[None, :])
    block = jnp.concatenate([placed, count_tile], axis=0)
    slots = jnp.arange(pairs.shape[3], dtype=jnp.int32)
    table = jnp.where(slots[None, :] < pair_count[0, 0], pairs[0, 0], -1000000).reshape(8, 128)

    rows = block.shape[0]
    total = n_scan * n_cad
    gathered, masks, all_counts = pl.pallas_call(
        functools.partial(gather_kernel, n_scan, n_cad, n_cad * blocks),
        out_shape=(
            jax.ShapeDtypeStruct((n_cad, n_scan, rows, SUB, 128), jnp.float32),
            jax.ShapeDtypeStruct((n_scan, n_cad * blocks), jnp.int32),
            jax.ShapeDtypeStruct((total, 128), jnp.int32),
        ),
        in_specs=[VMEM, VMEM],
        out_specs=(VMEM, VMEM, VMEM),
        scratch_shapes=[
            pltpu.VMEM((n_scan, 8, 128), jnp.int32),
            DMA((n_scan,)), DMA((n_scan,)), DMA((n_scan,)), DMA((n_scan,)),
            DMA((n_hi, n_scan)), DMA((n_hi, n_scan)), DMA((n_hi, n_scan)), DMA((n_hi, n_scan)),
            DMA, DMA,
        ],
        compiler_params=pltpu.CompilerParams(collective_id=0, has_side_effects=True, vmem_limit_bytes=LIMIT),
        name="gather_points",
    )(block, table)

    parts, tri_out = pl.pallas_call(
        functools.partial(pairs_kernel, n_scan, n_cad),
        out_shape=(
            jax.ShapeDtypeStruct((total, halves, SUB, 128), jnp.float32),
            jax.ShapeDtypeStruct((8, 128), jnp.float32),
        ),
        in_specs=[SMEM, SMEM, VMEM, VMEM],
        out_specs=(VMEM, VMEM),
        scratch_shapes=[
            pltpu.VMEM((N_ROWS, 8, 128), jnp.float32),
            pltpu.VMEM((8, SUB, 128), jnp.float32),
        ],
        compiler_params=pltpu.CompilerParams(vmem_limit_bytes=LIMIT),
        name="listed_pairs",
    )(masks, all_counts, gathered.reshape(total, rows, SUB, 128), triangles.reshape(9, 8, 128))

    own = pl.pallas_call(
        functools.partial(reduce_kernel, n_scan, n_cad),
        out_shape=jax.ShapeDtypeStruct((halves, SUB, 128), jnp.float32),
        in_specs=[VMEM],
        out_specs=VMEM,
        scratch_shapes=[
            pltpu.VMEM((n_cad, n_scan, halves, SUB, 128), jnp.float32),
            pltpu.VMEM((n_scan, halves, SUB, 128), jnp.float32),
            pltpu.VMEM((n_scan, halves, SUB, 128), jnp.float32),
            DMA((n_cad,)), DMA((n_cad,)), DMA((n_scan,)), DMA((n_scan,)),
        ],
        compiler_params=pltpu.CompilerParams(collective_id=1, has_side_effects=True, vmem_limit_bytes=LIMIT),
        name="reduce_points",
    )(parts.reshape(n_cad, n_scan, halves, SUB, 128))
    nearest = own.reshape(halves, SUB, PACK, GROUPS).transpose(0, 2, 3, 1).reshape(1, share)
    point_out = jnp.where(valid.reshape(1, share), nearest, 0.0)
    return point_out, tri_out.reshape(1, 8 * 128)


def solution(mesh):
    return jax.shard_map(
        functools.partial(shards, mesh.shape["scan"], mesh.shape["cad"]),
        mesh=mesh,
        in_specs=(
            P(None, "scan", "cad"),
            P(None, "cad", "scan"),
            P("scan", "cad"),
            P("scan", "cad", None, None),
            P("scan", "cad"),
        ),
        out_specs=(P("scan", "cad"), P("cad", "scan")),
        check_vma=False,
    )
```

```python
import functools

import jax
import jax.numpy as jnp
from jax import lax
from jax.experimental import pallas as pl
from jax.experimental.pallas import tpu as pltpu
from jax.sharding import PartitionSpec as P

PBLK = 256
TBLK = 128
SUB = 8
PACK = SUB * 128 // PBLK
UNROLL = 16

far_value = 1e30
away = 1e4

MESH = pl.DeviceIdType.MESH


def gather_kernel(
    n_scan, n_cad, n_blocks, block_ref, list_ref, all_ref, mask_ref, count_ref,
    lists, scan_send, scan_recv, list_send, list_recv, hi_send, hi_recv, core_send, core_recv, own_sem, own_list_sem,
):
    n_hi = n_cad // 2
    s = lax.axis_index("scan")
    c = lax.axis_index("cad")
    hi = c // 2
    core = c % 2

    def hi_peer(j):
        return lax.rem(hi + j, n_hi) * 2 + core

    sibling = hi * 2 + (1 - core)

    barrier = pltpu.get_barrier_semaphore()
    for k in range(1, n_scan):
        pl.semaphore_signal(barrier, inc=1, device_id=(lax.rem(s + k, n_scan), c), device_id_type=MESH)
    for j in range(1, n_hi):
        pl.semaphore_signal(barrier, inc=1, device_id=(s, hi_peer(j)), device_id_type=MESH)
    pl.semaphore_signal(barrier, inc=1, device_id=(s, sibling), device_id_type=MESH)
    own = pltpu.make_async_copy(block_ref, all_ref.at[c, s], own_sem)
    own.start()
    own_list = pltpu.make_async_copy(list_ref, lists.at[s], own_list_sem)
    own_list.start()
    pl.semaphore_wait(barrier, n_scan - 1 + n_hi - 1 + 1)

    sends = []

    def remote(src, dst, send, recv, device):
        copy = pltpu.make_async_remote_copy(
            src_ref=src, dst_ref=dst, send_sem=send, recv_sem=recv, device_id=device, device_id_type=MESH
        )
        return copy

    scan_copies = []
    for k in range(1, n_scan):
        copy = remote(block_ref, all_ref.at[c, s], scan_send.at[k], scan_recv.at[k], (lax.rem(s + k, n_scan), c))
        copy.start()
        sends.append(copy)
        scan_copies.append(copy)
    hi_copies = {}

    def forward(k, src, source_scan):
        for j in range(1, n_hi):
            copy = remote(
                src, all_ref.at[c, source_scan], hi_send.at[j, k], hi_recv.at[j, k], (s, hi_peer(j))
            )
            copy.start()
            sends.append(copy)
            hi_copies[(j, k)] = copy
        copy = remote(src, all_ref.at[c, source_scan], core_send.at[0, k], core_recv.at[0, k], (s, sibling))
        copy.start()
        sends.append(copy)
        core_copies.append(copy)

    core_copies = []
    forward(0, block_ref, s)
    list_copies = []
    for k in range(1, n_scan):
        copy = remote(list_ref, lists.at[s], list_send.at[k], list_recv.at[k], (lax.rem(s + k, n_scan), c))
        copy.start()
        sends.append(copy)
        list_copies.append(copy)
    for k in range(1, n_scan):
        scan_copies[k - 1].wait_recv()
        source = lax.rem(s + n_scan - k, n_scan)
        forward(k, all_ref.at[c, source], source)

    own_list.wait()
    for copy in list_copies:
        copy.wait_recv()
    n_tri = 8
    first = s * n_tri
    for shard in range(n_scan):
        total = jnp.zeros((n_tri, n_blocks), jnp.float32)
        for part in range(4):
            point_row = lists[shard, part : part + 1, :]
            tri_row = lists[shard, part + 4 : part + 5, :] - first
            points_hot = (lax.broadcasted_iota(jnp.int32, (n_blocks, 128), 0) == point_row).astype(jnp.float32)
            tris_hot = (lax.broadcasted_iota(jnp.int32, (n_tri, 128), 0) == tri_row).astype(jnp.float32)
            total += lax.dot_general(
                tris_hot, points_hot, (((1,), (1,)), ((), ())), preferred_element_type=jnp.float32
            )
        bit = jnp.left_shift(1, lax.broadcasted_iota(jnp.int32, (n_tri, n_blocks), 0))
        bits = jnp.where(total > 0.5, bit, 0)
        mask_ref[shard : shard + 1, :] = jnp.sum(bits, axis=0, keepdims=True)

    for j in range(1, n_hi):
        column = lax.rem(hi + n_hi - j, n_hi) * 2 + core
        for k in range(n_scan):
            hi_copies[(j, k)].wait_recv()
            source = lax.rem(s + n_scan - k, n_scan)
            src = all_ref.at[column, source]
            copy = remote(src, all_ref.at[column, source], core_send.at[j, k], core_recv.at[j, k], (s, sibling))
            copy.start()
            sends.append(copy)
            core_copies.append(copy)
    for copy in core_copies:
        copy.wait_recv()
    own.wait()
    for copy in sends:
        copy.wait_send()
    for column in range(n_cad):
        for shard in range(n_scan):
            row = column * n_scan + shard
            count_ref[row : row + 1, :] = all_ref[column, shard, 6, 0:1, :].astype(jnp.int32)


def reduce_kernel(n_scan, n_cad, part_ref, out_ref, first, held, second, first_send, first_recv, second_send, second_recv):
    s = lax.axis_index("scan")
    c = lax.axis_index("cad")
    barrier = pltpu.get_barrier_semaphore()
    for k in range(1, n_scan):
        pl.semaphore_signal(barrier, inc=1, device_id=(lax.rem(s + k, n_scan), c), device_id_type=MESH)
    for k in range(1, n_cad):
        pl.semaphore_signal(barrier, inc=1, device_id=(s, lax.rem(c + k, n_cad)), device_id_type=MESH)
    pl.semaphore_wait(barrier, n_scan - 1 + n_cad - 1)
    copies = []
    for k in range(1, n_cad):
        column = lax.rem(c + k, n_cad)
        copy = pltpu.make_async_remote_copy(
            src_ref=part_ref.at[column], dst_ref=first.at[k], send_sem=first_send.at[k], recv_sem=first_recv.at[k],
            device_id=(s, column), device_id_type=MESH,
        )
        copy.start()
        copies.append(copy)
    for copy in copies:
        copy.wait_recv()
    total = part_ref[c]
    for k in range(1, n_cad):
        total = jnp.minimum(total, first[k])
    held[...] = total
    later = []
    for k in range(1, n_scan):
        row = lax.rem(s + k, n_scan)
        copy = pltpu.make_async_remote_copy(
            src_ref=held.at[row], dst_ref=second.at[k], send_sem=second_send.at[k], recv_sem=second_recv.at[k],
            device_id=(row, c), device_id_type=MESH,
        )
        copy.start()
        later.append(copy)
    for copy in later:
        copy.wait_recv()
    own = held[s]
    for k in range(1, n_scan):
        own = jnp.minimum(own, second[k])
    out_ref[...] = own
    for copy in copies + later:
        copy.wait_send()


def dot3(left, right):
    return left[0] * right[0] + left[1] * right[1] + left[2] * right[2]


def minus(left, right):
    return [left[i] - right[i] for i in range(3)]


def frame_rows(tri_ref):
    a = [tri_ref[i] for i in range(3)]
    b = [tri_ref[3 + i] for i in range(3)]
    far = [tri_ref[6 + i] for i in range(3)]
    e0 = minus(b, a)
    h = minus(far, a)
    base = jnp.sqrt(dot3(e0, e0))
    u = [x / base for x in e0]
    cx = dot3(h, u)
    h = [h[i] - cx * u[i] for i in range(3)]
    again = dot3(h, u)
    h = [h[i] - again * u[i] for i in range(3)]
    cx = cx + again
    cy = jnp.sqrt(dot3(h, h))
    v = [x / cy for x in h]
    w = [u[1] * v[2] - u[2] * v[1], u[2] * v[0] - u[0] * v[2], u[0] * v[1] - u[1] * v[0]]
    dx = cx - base
    len1 = jnp.sqrt(dx * dx + cy * cy)
    len2 = jnp.sqrt(cx * cx + cy * cy)
    return a + u + v + w + [base, dx / len1, cy / len1, len1, cx / len2, cy / len2, len2]


N_ROWS = 19


def tile_distance(points, rows):
    ax, ay, az, u0, u1, u2, v0, v1, v2, w0, w1, w2, base, d0, d1, len1, f0, f1, len2 = rows
    px, py, pz = points
    px = px - ax
    py = py - ay
    pz = pz - az
    x = px * u0 + py * u1 + pz * u2
    y = px * v0 + py * v1 + pz * v2
    z = px * w0 + py * w1 + pz * w2
    gap0 = x - jnp.minimum(jnp.maximum(x, 0.0), base)
    seg0 = gap0 * gap0 + y * y
    xb = x - base
    along1 = xb * d0 + y * d1
    side1 = y * d0 - xb * d1
    gap1 = along1 - jnp.minimum(jnp.maximum(along1, 0.0), len1)
    seg1 = gap1 * gap1 + side1 * side1
    along2 = x * f0 + y * f1
    side2 = x * f1 - y * f0
    gap2 = along2 - jnp.minimum(jnp.maximum(along2, 0.0), len2)
    seg2 = gap2 * gap2 + side2 * side2
    edges = jnp.minimum(jnp.minimum(seg0, seg1), seg2)
    side = jnp.minimum(jnp.minimum(y, side1), side2)
    return z * z + jnp.where(side >= 0.0, 0.0, edges)


def pairs_kernel(n_scan, n_cad, mask_ref, count_ref, all_ref, tri_ref, part_ref, out_ref, frames, wide, tri_acc):
    for i, row in enumerate(frame_rows(tri_ref)):
        frames[i] = row

    def widen(i, carry):
        for t in range(8):
            wide[i, t * TBLK : (t + 1) * TBLK, :] = jnp.broadcast_to(frames[i, t : t + 1, :], (TBLK, 128)).T
        return carry

    lax.fori_loop(0, N_ROWS, widen, 0)
    part_ref[...] = jnp.full_like(part_ref, far_value)
    tri_acc[...] = jnp.full_like(tri_acc, far_value)

    def per_block(index, carry):
        where = index // 8
        slot = index % 8
        mask = mask_ref[where % n_scan, (where // n_scan) * 8 + slot]
        half = slot // PACK
        first = (slot % PACK) * 2

        def visit(chunks):
            points = [
                tuple(
                    jnp.broadcast_to(all_ref[where, 2 * i + half, pl.ds(first + q, 1), :], (SUB, 128))
                    for i in range(3)
                )
                for q in range(chunks)
            ]

            def per_tri(state):
                left, nearest = state
                tri = 31 - lax.clz(left)

                def body(step, nearest):
                    at = pl.ds(pl.multiple_of(tri * TBLK + step * SUB, SUB), SUB)
                    rows = [wide[i, at, :] for i in range(N_ROWS)]
                    best = tri_acc[at, :]
                    out = []
                    for q in range(chunks):
                        dist = tile_distance(points[q], rows)
                        best = jnp.minimum(best, dist)
                        out.append(jnp.minimum(nearest[q], dist))
                    tri_acc[at, :] = best
                    return tuple(out)

                nearest = lax.fori_loop(0, TBLK // SUB, body, nearest, unroll=UNROLL)
                return left - jnp.left_shift(1, tri), nearest

            start = tuple(jnp.full((SUB, 128), far_value, jnp.float32) for _ in range(chunks))
            _, nearest = lax.while_loop(lambda state: state[0] != 0, per_tri, (mask, start))
            for q in range(chunks):
                part_ref[where, half, pl.ds(first + q, 1), :] = jnp.min(nearest[q], axis=0, keepdims=True)

        @pl.when(mask != 0)
        def _():
            count = count_ref[where, slot]
            pl.when(count <= 128)(lambda: visit(1))
            pl.when(count > 128)(lambda: visit(2))

        return carry

    lax.fori_loop(0, n_scan * n_cad * 8, per_block, 0)
    for t in range(8):
        out_ref[t : t + 1, :] = jnp.min(tri_acc[t * TBLK : (t + 1) * TBLK, :].T, axis=0, keepdims=True)


VMEM = pl.BlockSpec(memory_space=pltpu.VMEM)
SMEM = pl.BlockSpec(memory_space=pltpu.SMEM)
DMA = pltpu.SemaphoreType.DMA
LIMIT = 40 * 1024 * 1024


def shards(n_scan, n_cad, points, triangles, point_count, pairs, pair_count):
    share = points.shape[2]
    blocks = share // PBLK
    n_hi = n_cad // 2
    halves = blocks // PACK
    counts = point_count[0]
    valid = jnp.arange(PBLK, dtype=jnp.int32)[None, :] < counts[:, None]
    placed = jnp.where(valid[None], points[:, 0].reshape(3, blocks, PBLK), away)
    placed = placed.reshape(3 * halves, SUB, 128)
    count_tile = jnp.zeros((1, SUB, 128), jnp.float32).at[0, :, :blocks].set(counts.astype(jnp.float32)[None, :])
    block = jnp.concatenate([placed, count_tile], axis=0)
    slots = jnp.arange(pairs.shape[3], dtype=jnp.int32)
    table = jnp.where(slots[None, :] < pair_count[0, 0], pairs[0, 0], -1000000).reshape(8, 128)

    rows = block.shape[0]
    total = n_scan * n_cad
    gathered, masks, all_counts = pl.pallas_call(
        functools.partial(gather_kernel, n_scan, n_cad, n_cad * blocks),
        out_shape=(
            jax.ShapeDtypeStruct((n_cad, n_scan, rows, SUB, 128), jnp.float32),
            jax.ShapeDtypeStruct((n_scan, n_cad * blocks), jnp.int32),
            jax.ShapeDtypeStruct((total, 128), jnp.int32),
        ),
        in_specs=[VMEM, VMEM],
        out_specs=(VMEM, VMEM, VMEM),
        scratch_shapes=[
            pltpu.VMEM((n_scan, 8, 128), jnp.int32),
            DMA((n_scan,)), DMA((n_scan,)), DMA((n_scan,)), DMA((n_scan,)),
            DMA((n_hi, n_scan)), DMA((n_hi, n_scan)), DMA((n_hi, n_scan)), DMA((n_hi, n_scan)),
            DMA, DMA,
        ],
        compiler_params=pltpu.CompilerParams(collective_id=0, has_side_effects=True, vmem_limit_bytes=LIMIT),
        name="gather_points",
    )(block, table)

    parts, tri_out = pl.pallas_call(
        functools.partial(pairs_kernel, n_scan, n_cad),
        out_shape=(
            jax.ShapeDtypeStruct((total, halves, SUB, 128), jnp.float32),
            jax.ShapeDtypeStruct((8, 128), jnp.float32),
        ),
        in_specs=[SMEM, SMEM, VMEM, VMEM],
        out_specs=(VMEM, VMEM),
        scratch_shapes=[
            pltpu.VMEM((N_ROWS, 8, 128), jnp.float32),
            pltpu.VMEM((N_ROWS, 8 * TBLK, 128), jnp.float32),
            pltpu.VMEM((8 * TBLK, 128), jnp.float32),
        ],
        compiler_params=pltpu.CompilerParams(vmem_limit_bytes=LIMIT),
        name="listed_pairs",
    )(masks, all_counts, gathered.reshape(total, rows, SUB, 128), triangles.reshape(9, 8, 128))

    own = pl.pallas_call(
        functools.partial(reduce_kernel, n_scan, n_cad),
        out_shape=jax.ShapeDtypeStruct((halves, SUB, 128), jnp.float32),
        in_specs=[VMEM],
        out_specs=VMEM,
        scratch_shapes=[
            pltpu.VMEM((n_cad, n_scan, halves, SUB, 128), jnp.float32),
            pltpu.VMEM((n_scan, halves, SUB, 128), jnp.float32),
            pltpu.VMEM((n_scan, halves, SUB, 128), jnp.float32),
            DMA((n_cad,)), DMA((n_cad,)), DMA((n_scan,)), DMA((n_scan,)),
        ],
        compiler_params=pltpu.CompilerParams(collective_id=1, has_side_effects=True, vmem_limit_bytes=LIMIT),
        name="reduce_points",
    )(parts.reshape(n_cad, n_scan, halves, SUB, 128))
    nearest = own.reshape(1, share)
    point_out = jnp.where(valid.reshape(1, share), nearest, 0.0)
    return point_out, tri_out.reshape(1, 8 * 128)


def solution(mesh):
    return jax.shard_map(
        functools.partial(shards, mesh.shape["scan"], mesh.shape["cad"]),
        mesh=mesh,
        in_specs=(
            P(None, "scan", "cad"),
            P(None, "cad", "scan"),
            P("scan", "cad"),
            P("scan", "cad", None, None),
            P("scan", "cad"),
        ),
        out_specs=(P("scan", "cad"), P("cad", "scan")),
        check_vma=False,
    )
```

```python
import functools

import jax
import jax.numpy as jnp
from jax import lax
from jax.experimental import pallas as pl
from jax.experimental.pallas import tpu as pltpu
from jax.sharding import PartitionSpec as P

PBLK = 256
TBLK = 128
SUB = 8
PACK = SUB * 128 // PBLK
UNROLL = 16

far_value = 1e30
away = 1e4

MESH = pl.DeviceIdType.MESH


def gather_kernel(
    n_scan, n_cad, n_blocks, block_ref, list_ref, all_ref, mask_ref, count_ref,
    lists, scan_send, scan_recv, list_send, list_recv, hi_send, hi_recv, core_send, core_recv, own_sem, own_list_sem,
):
    n_hi = n_cad // 2
    s = lax.axis_index("scan")
    c = lax.axis_index("cad")
    hi = c // 2
    core = c % 2

    def hi_peer(j):
        return lax.rem(hi + j, n_hi) * 2 + core

    sibling = hi * 2 + (1 - core)

    barrier = pltpu.get_barrier_semaphore()
    for k in range(1, n_scan):
        pl.semaphore_signal(barrier, inc=1, device_id=(lax.rem(s + k, n_scan), c), device_id_type=MESH)
    for j in range(1, n_hi):
        pl.semaphore_signal(barrier, inc=1, device_id=(s, hi_peer(j)), device_id_type=MESH)
    pl.semaphore_signal(barrier, inc=1, device_id=(s, sibling), device_id_type=MESH)
    own = pltpu.make_async_copy(block_ref, all_ref.at[c, s], own_sem)
    own.start()
    own_list = pltpu.make_async_copy(list_ref, lists.at[s], own_list_sem)
    own_list.start()
    pl.semaphore_wait(barrier, n_scan - 1 + n_hi - 1 + 1)

    sends = []

    def remote(src, dst, send, recv, device):
        copy = pltpu.make_async_remote_copy(
            src_ref=src, dst_ref=dst, send_sem=send, recv_sem=recv, device_id=device, device_id_type=MESH
        )
        return copy

    scan_copies = []
    for k in range(1, n_scan):
        copy = remote(block_ref, all_ref.at[c, s], scan_send.at[k], scan_recv.at[k], (lax.rem(s + k, n_scan), c))
        copy.start()
        sends.append(copy)
        scan_copies.append(copy)
    hi_copies = {}

    def forward(k, src, source_scan):
        for j in range(1, n_hi):
            copy = remote(
                src, all_ref.at[c, source_scan], hi_send.at[j, k], hi_recv.at[j, k], (s, hi_peer(j))
            )
            copy.start()
            sends.append(copy)
            hi_copies[(j, k)] = copy
        copy = remote(src, all_ref.at[c, source_scan], core_send.at[0, k], core_recv.at[0, k], (s, sibling))
        copy.start()
        sends.append(copy)
        core_copies.append(copy)

    core_copies = []
    forward(0, block_ref, s)
    list_copies = []
    for k in range(1, n_scan):
        copy = remote(list_ref, lists.at[s], list_send.at[k], list_recv.at[k], (lax.rem(s + k, n_scan), c))
        copy.start()
        sends.append(copy)
        list_copies.append(copy)
    for k in range(1, n_scan):
        scan_copies[k - 1].wait_recv()
        source = lax.rem(s + n_scan - k, n_scan)
        forward(k, all_ref.at[c, source], source)

    own_list.wait()
    for copy in list_copies:
        copy.wait_recv()
    n_tri = 8
    first = s * n_tri
    for shard in range(n_scan):
        total = jnp.zeros((n_tri, n_blocks), jnp.float32)
        for part in range(4):
            point_row = lists[shard, part : part + 1, :]
            tri_row = lists[shard, part + 4 : part + 5, :] - first
            points_hot = (lax.broadcasted_iota(jnp.int32, (n_blocks, 128), 0) == point_row).astype(jnp.float32)
            tris_hot = (lax.broadcasted_iota(jnp.int32, (n_tri, 128), 0) == tri_row).astype(jnp.float32)
            total += lax.dot_general(
                tris_hot, points_hot, (((1,), (1,)), ((), ())), preferred_element_type=jnp.float32
            )
        bit = jnp.left_shift(1, lax.broadcasted_iota(jnp.int32, (n_tri, n_blocks), 0))
        bits = jnp.where(total > 0.5, bit, 0)
        mask_ref[shard : shard + 1, :] = jnp.sum(bits, axis=0, keepdims=True)

    for j in range(1, n_hi):
        column = lax.rem(hi + n_hi - j, n_hi) * 2 + core
        for k in range(n_scan):
            hi_copies[(j, k)].wait_recv()
            source = lax.rem(s + n_scan - k, n_scan)
            src = all_ref.at[column, source]
            copy = remote(src, all_ref.at[column, source], core_send.at[j, k], core_recv.at[j, k], (s, sibling))
            copy.start()
            sends.append(copy)
            core_copies.append(copy)
    for copy in core_copies:
        copy.wait_recv()
    own.wait()
    for copy in sends:
        copy.wait_send()
    for column in range(n_cad):
        for shard in range(n_scan):
            row = column * n_scan + shard
            count_ref[row : row + 1, :] = all_ref[column, shard, 6, 0:1, :].astype(jnp.int32)


def reduce_kernel(n_scan, n_cad, part_ref, out_ref, first, held, second, first_send, first_recv, second_send, second_recv):
    s = lax.axis_index("scan")
    c = lax.axis_index("cad")
    barrier = pltpu.get_barrier_semaphore()
    for k in range(1, n_scan):
        pl.semaphore_signal(barrier, inc=1, device_id=(lax.rem(s + k, n_scan), c), device_id_type=MESH)
    for k in range(1, n_cad):
        pl.semaphore_signal(barrier, inc=1, device_id=(s, lax.rem(c + k, n_cad)), device_id_type=MESH)
    pl.semaphore_wait(barrier, n_scan - 1 + n_cad - 1)
    copies = []
    for k in range(1, n_cad):
        column = lax.rem(c + k, n_cad)
        copy = pltpu.make_async_remote_copy(
            src_ref=part_ref.at[column], dst_ref=first.at[k], send_sem=first_send.at[k], recv_sem=first_recv.at[k],
            device_id=(s, column), device_id_type=MESH,
        )
        copy.start()
        copies.append(copy)
    for copy in copies:
        copy.wait_recv()
    total = part_ref[c]
    for k in range(1, n_cad):
        total = jnp.minimum(total, first[k])
    held[...] = total
    later = []
    for k in range(1, n_scan):
        row = lax.rem(s + k, n_scan)
        copy = pltpu.make_async_remote_copy(
            src_ref=held.at[row], dst_ref=second.at[k], send_sem=second_send.at[k], recv_sem=second_recv.at[k],
            device_id=(row, c), device_id_type=MESH,
        )
        copy.start()
        later.append(copy)
    for copy in later:
        copy.wait_recv()
    own = held[s]
    for k in range(1, n_scan):
        own = jnp.minimum(own, second[k])
    out_ref[...] = own
    for copy in copies + later:
        copy.wait_send()


def dot3(left, right):
    return left[0] * right[0] + left[1] * right[1] + left[2] * right[2]


def minus(left, right):
    return [left[i] - right[i] for i in range(3)]


def frame_rows(tri_ref):
    a = [tri_ref[i] for i in range(3)]
    b = [tri_ref[3 + i] for i in range(3)]
    far = [tri_ref[6 + i] for i in range(3)]
    e0 = minus(b, a)
    h = minus(far, a)
    base = jnp.sqrt(dot3(e0, e0))
    u = [x / base for x in e0]
    cx = dot3(h, u)
    h = [h[i] - cx * u[i] for i in range(3)]
    again = dot3(h, u)
    h = [h[i] - again * u[i] for i in range(3)]
    cx = cx + again
    cy = jnp.sqrt(dot3(h, h))
    v = [x / cy for x in h]
    w = [u[1] * v[2] - u[2] * v[1], u[2] * v[0] - u[0] * v[2], u[0] * v[1] - u[1] * v[0]]
    dx = cx - base
    len1 = jnp.sqrt(dx * dx + cy * cy)
    len2 = jnp.sqrt(cx * cx + cy * cy)
    return a + u + v + w + [base, dx / len1, cy / len1, len1, cx / len2, cy / len2, len2]


N_ROWS = 19


def tile_distance(points, rows):
    ax, ay, az, u0, u1, u2, v0, v1, v2, w0, w1, w2, base, d0, d1, len1, f0, f1, len2 = rows
    px, py, pz = points
    px = px - ax
    py = py - ay
    pz = pz - az
    x = px * u0 + py * u1 + pz * u2
    y = px * v0 + py * v1 + pz * v2
    z = px * w0 + py * w1 + pz * w2
    gap0 = x - jnp.minimum(jnp.maximum(x, 0.0), base)
    seg0 = gap0 * gap0 + y * y
    xb = x - base
    along1 = xb * d0 + y * d1
    side1 = y * d0 - xb * d1
    gap1 = along1 - jnp.minimum(jnp.maximum(along1, 0.0), len1)
    seg1 = gap1 * gap1 + side1 * side1
    along2 = x * f0 + y * f1
    side2 = x * f1 - y * f0
    gap2 = along2 - jnp.minimum(jnp.maximum(along2, 0.0), len2)
    seg2 = gap2 * gap2 + side2 * side2
    edges = jnp.minimum(jnp.minimum(seg0, seg1), seg2)
    side = jnp.minimum(jnp.minimum(y, side1), side2)
    return z * z + jnp.where(side >= 0.0, 0.0, edges)


def pairs_kernel(n_scan, n_cad, mask_ref, count_ref, all_ref, tri_ref, part_ref, out_ref, frames, wide, tri_acc):
    for i, row in enumerate(frame_rows(tri_ref)):
        frames[i] = row

    def widen(i, carry):
        for t in range(8):
            wide[i, t * TBLK : (t + 1) * TBLK, :] = jnp.broadcast_to(frames[i, t : t + 1, :], (TBLK, 128)).T
        return carry

    lax.fori_loop(0, N_ROWS, widen, 0, unroll=True)
    part_ref[...] = jnp.full_like(part_ref, far_value)
    tri_acc[...] = jnp.full_like(tri_acc, far_value)

    def per_block(index, carry):
        where = index // 8
        slot = index % 8
        mask = mask_ref[where % n_scan, (where // n_scan) * 8 + slot]
        half = slot // PACK
        first = (slot % PACK) * 2

        def visit(chunks):
            points = [
                tuple(
                    jnp.broadcast_to(all_ref[where, 2 * i + half, pl.ds(first + q, 1), :], (SUB, 128))
                    for i in range(3)
                )
                for q in range(chunks)
            ]

            def per_tri(state):
                left, nearest = state
                tri = 31 - lax.clz(left)

                def body(step, nearest):
                    at = pl.ds(pl.multiple_of(tri * TBLK + step * SUB, SUB), SUB)
                    rows = [wide[i, at, :] for i in range(N_ROWS)]
                    best = tri_acc[at, :]
                    out = []
                    for q in range(chunks):
                        dist = tile_distance(points[q], rows)
                        best = jnp.minimum(best, dist)
                        out.append(jnp.minimum(nearest[q], dist))
                    tri_acc[at, :] = best
                    return tuple(out)

                nearest = lax.fori_loop(0, TBLK // SUB, body, nearest, unroll=UNROLL)
                return left - jnp.left_shift(1, tri), nearest

            start = tuple(jnp.full((SUB, 128), far_value, jnp.float32) for _ in range(chunks))
            _, nearest = lax.while_loop(lambda state: state[0] != 0, per_tri, (mask, start))
            for q in range(chunks):
                part_ref[where, half, pl.ds(first + q, 1), :] = jnp.min(nearest[q], axis=0, keepdims=True)

        @pl.when(mask != 0)
        def _():
            count = count_ref[where, slot]
            pl.when(count <= 128)(lambda: visit(1))
            pl.when(count > 128)(lambda: visit(2))

        return carry

    lax.fori_loop(0, n_scan * n_cad * 8, per_block, 0)
    for t in range(8):
        out_ref[t : t + 1, :] = jnp.min(tri_acc[t * TBLK : (t + 1) * TBLK, :].T, axis=0, keepdims=True)


VMEM = pl.BlockSpec(memory_space=pltpu.VMEM)
SMEM = pl.BlockSpec(memory_space=pltpu.SMEM)
DMA = pltpu.SemaphoreType.DMA
LIMIT = 40 * 1024 * 1024


def shards(n_scan, n_cad, points, triangles, point_count, pairs, pair_count):
    share = points.shape[2]
    blocks = share // PBLK
    n_hi = n_cad // 2
    halves = blocks // PACK
    counts = point_count[0]
    valid = jnp.arange(PBLK, dtype=jnp.int32)[None, :] < counts[:, None]
    placed = jnp.where(valid[None], points[:, 0].reshape(3, blocks, PBLK), away)
    placed = placed.reshape(3 * halves, SUB, 128)
    count_tile = jnp.zeros((1, SUB, 128), jnp.float32).at[0, :, :blocks].set(counts.astype(jnp.float32)[None, :])
    block = jnp.concatenate([placed, count_tile], axis=0)
    slots = jnp.arange(pairs.shape[3], dtype=jnp.int32)
    table = jnp.where(slots[None, :] < pair_count[0, 0], pairs[0, 0], -1000000).reshape(8, 128)

    rows = block.shape[0]
    total = n_scan * n_cad
    gathered, masks, all_counts = pl.pallas_call(
        functools.partial(gather_kernel, n_scan, n_cad, n_cad * blocks),
        out_shape=(
            jax.ShapeDtypeStruct((n_cad, n_scan, rows, SUB, 128), jnp.float32),
            jax.ShapeDtypeStruct((n_scan, n_cad * blocks), jnp.int32),
            jax.ShapeDtypeStruct((total, 128), jnp.int32),
        ),
        in_specs=[VMEM, VMEM],
        out_specs=(VMEM, VMEM, VMEM),
        scratch_shapes=[
            pltpu.VMEM((n_scan, 8, 128), jnp.int32),
            DMA((n_scan,)), DMA((n_scan,)), DMA((n_scan,)), DMA((n_scan,)),
            DMA((n_hi, n_scan)), DMA((n_hi, n_scan)), DMA((n_hi, n_scan)), DMA((n_hi, n_scan)),
            DMA, DMA,
        ],
        compiler_params=pltpu.CompilerParams(collective_id=0, has_side_effects=True, vmem_limit_bytes=LIMIT),
        name="gather_points",
    )(block, table)

    parts, tri_out = pl.pallas_call(
        functools.partial(pairs_kernel, n_scan, n_cad),
        out_shape=(
            jax.ShapeDtypeStruct((total, halves, SUB, 128), jnp.float32),
            jax.ShapeDtypeStruct((8, 128), jnp.float32),
        ),
        in_specs=[SMEM, SMEM, VMEM, VMEM],
        out_specs=(VMEM, VMEM),
        scratch_shapes=[
            pltpu.VMEM((N_ROWS, 8, 128), jnp.float32),
            pltpu.VMEM((N_ROWS, 8 * TBLK, 128), jnp.float32),
            pltpu.VMEM((8 * TBLK, 128), jnp.float32),
        ],
        compiler_params=pltpu.CompilerParams(vmem_limit_bytes=LIMIT),
        name="listed_pairs",
    )(masks, all_counts, gathered.reshape(total, rows, SUB, 128), triangles.reshape(9, 8, 128))

    own = pl.pallas_call(
        functools.partial(reduce_kernel, n_scan, n_cad),
        out_shape=jax.ShapeDtypeStruct((halves, SUB, 128), jnp.float32),
        in_specs=[VMEM],
        out_specs=VMEM,
        scratch_shapes=[
            pltpu.VMEM((n_cad, n_scan, halves, SUB, 128), jnp.float32),
            pltpu.VMEM((n_scan, halves, SUB, 128), jnp.float32),
            pltpu.VMEM((n_scan, halves, SUB, 128), jnp.float32),
            DMA((n_cad,)), DMA((n_cad,)), DMA((n_scan,)), DMA((n_scan,)),
        ],
        compiler_params=pltpu.CompilerParams(collective_id=1, has_side_effects=True, vmem_limit_bytes=LIMIT),
        name="reduce_points",
    )(parts.reshape(n_cad, n_scan, halves, SUB, 128))
    nearest = own.reshape(1, share)
    point_out = jnp.where(valid.reshape(1, share), nearest, 0.0)
    return point_out, tri_out.reshape(1, 8 * 128)


def solution(mesh):
    return jax.shard_map(
        functools.partial(shards, mesh.shape["scan"], mesh.shape["cad"]),
        mesh=mesh,
        in_specs=(
            P(None, "scan", "cad"),
            P(None, "cad", "scan"),
            P("scan", "cad"),
            P("scan", "cad", None, None),
            P("scan", "cad"),
        ),
        out_specs=(P("scan", "cad"), P("cad", "scan")),
        check_vma=False,
    )
```
